128 devices in a mesh: grp: 2 (over core), own: 64 (over y, z, x).
Axes of the slice: x: 4, y: 4, z: 4, core: 2. Of those that a mesh axis runs over, the one named last changes fastest.
Arguments:
- row_x: bfloat16 [131072, 1024], P(('grp', 'own')), parts along dimension 0, may hold values from -6 to 6
- row_user: int32 [131072, 1], P(('grp', 'own')), parts along dimension 0, may hold values from 0 to 63; in each aligned block of 1024 rows (0 to 1023, 1024 to 2047, ...) at most 32 rows name the same one
- user_owner: int32 [128], P('grp'), parts along dimension 0, may hold values from 0 to 63, each once
- hist_len: int32 [128], P(('grp', 'own')), parts along dimension 0, may hold values from 1 to 1024, 32768 in all
- new_rows: bfloat16 [128, 64, 1024], P(('grp', 'own')), parts along dimension 0, may hold values from -6 to 6
- cache_keys: bfloat16 [128, 1024, 1024], P(('grp', 'own')), parts along dimension 0, may hold values from -6 to 6
- cache_values: bfloat16 [128, 1024, 1024], P(('grp', 'own')), parts along dimension 0, may hold values from -6 to 6
- w_in: bfloat16 [1024, 4096], replicated, may hold values from -0.1875 to 0.1875
- w_out: bfloat16 [1024, 1024], replicated, may hold values from -0.1875 to 0.1875
- w_score: float32 [1024], replicated, may hold values from -0.1875 to 0.1875
Outputs:
- scores: float32 [131072], P(('grp', 'own')), parts along dimension 0
- new_out: bfloat16 [128, 64, 1024], P(('grp', 'own')), parts along dimension 0
The draws below stay inside these ranges and needn't reach their ends.
There are 2 independent parts, one for each index of `grp`. The reference program is written for one: setup_inputs(seed, part) draws one part's arguments, and reference() takes and returns one part's arrays. A program takes and returns all parts, laid end to end along the dimension named above; an argument that names none is the same for every part. Nothing has to cross between parts.
Inputs may be any that keep to these rules, and one draw needn't show every extreme that they name: `row_user`: among the rows of one device no user appears more than 32 times, and some user appears exactly 32 times. `user_owner`: each device index appears once.
All inputs are finite; a program needn't handle non-finite values. No bound on the sum of `hist_len` on one device may be relied on, other than what follows from the above.
Results may differ from the reference program's by a relative error of at most 0.0095.
Values may be sent and summed in bfloat16 or wider, within the bound.
No kernel may reach another device: no remote copies, remote signals or barrier semaphores. Data moves between devices by JAX's collectives and lax.ppermute only.
A program may use at most 128 MiB of HBM per device.

```python
import math
import jax
import jax.numpy as jnp
import numpy as np
from jax import lax

D = 1024
HEADS = 8
NEW = 64
HIST = 1024
ROWS_DEV = 1024
USERS = 64
CAP = 32
ROWS = 65536
N_OWN = 64


def level_of(key, shape, split, smallest, high):
    def one(position, parts):
        steps = jax.random.uniform(jax.random.fold_in(jax.random.fold_in(key, 6), position), (parts,), jnp.float32, smallest / len(split), high / len(split))
        return jnp.repeat(jnp.exp(steps), shape[position] // parts).reshape((-1,) + (1,) * (len(shape) - position - 1))

    level = one(*split[0])
    for cut in split[1:]:
        level = level * one(*cut)
    return level


def profile(amount, total, limit, skew):
    loads = [(1 << 20) // math.isqrt(standing ** skew) + 1 for standing in range(2, amount + 1)]
    surplus, given = total - limit - (amount - 1), [1] * (amount - 1)
    while surplus > 0:
        movable = [i for i in range(amount - 1) if given[i] < limit]
        mass, left = sum([loads[i] for i in movable]), surplus
        for i in movable:
            more = min(limit - given[i], max(1, left * loads[i] // mass), surplus)
            given[i] = given[i] + more
            surplus = surplus - more
    return np.array([limit] + given)


def ragged_sizes(own_key, amount, total, most, slope):
    if amount == 2:
        one = jax.random.randint(own_key, (), max(1, total - most), min(most, total - 1) + 1)
        return jnp.stack([one, total - one])
    lengths = jnp.asarray(profile(amount, total, most, slope), jnp.int32)
    pairs = (amount - 1) // 2
    giver, taker = lengths[1:1 + 2 * pairs:2], lengths[2:2 + 2 * pairs:2]
    slack = jnp.minimum(giver - 1, most - taker)
    passed = jax.random.randint(jax.random.fold_in(own_key, 1), (pairs,), 0, 1 << 20) % (slack + 1)
    lengths = lengths.at[1:1 + 2 * pairs:2].set(giver - passed).at[2:2 + 2 * pairs:2].set(taker + passed)
    return lengths[jax.random.permutation(jax.random.fold_in(own_key, 2), amount)]


def routed_block(own_key, own, number, rows, count, top, bound, lean):
    order = jax.random.permutation(own_key, count)
    crowded, usual = portions_of(count, rows * top, bound, lean, True), portions_of(count, rows * top, bound, lean, False)
    places = jnp.arange(count)

    def named(sizes, turn):
        used = int((sizes > 0).sum())
        fixed = max(1, used // 4)
        moved = fixed + (places - fixed + turn * (used - fixed)) % max(1, count - fixed)
        return jnp.zeros((count,), jnp.int32).at[order[jnp.where(places < fixed, places, moved)]].set(jnp.asarray(sizes, jnp.int32))

    sizes = jnp.where(number % 4 == 0, named(crowded, number // 4), named(usual, number - number // 4 - 1))
    mixed = jax.random.permutation(jax.random.fold_in(own, 3), count)
    source_of, taker = mixed[0:count // 2 * 2:2], mixed[1:count // 2 * 2:2]
    margin = jnp.minimum(sizes[source_of] - 1, bound - sizes[taker]) // 2
    margin = jnp.where((source_of == order[0]) | (taker == order[0]) | (sizes[taker] == 0), 0, jnp.maximum(margin, 0))
    moved = jax.random.randint(jax.random.fold_in(own, 4), (count // 2,), 0, 1 << 20) % (margin + 1)
    sizes = sizes.at[source_of].add(-moved).at[taker].add(moved)
    members = jnp.searchsorted(jnp.cumsum(sizes), jnp.arange(rows * top), side="right").astype(jnp.int32)
    grid = members.reshape(top, rows).T
    grid = grid[jax.random.permutation(jax.random.fold_in(own, 1), rows)]
    turn = jax.random.randint(jax.random.fold_in(own, 2), (rows, 1), 0, top)
    return jnp.take_along_axis(grid, (jnp.arange(top)[None, :] + turn) % top, axis=1)


def portions_of(number_of, total, bound, skew, full):
    loads = [(1 << 20) // math.isqrt(rank ** skew) + 1 for rank in range(1, number_of + 1)]
    largest = bound if full else min(bound, max(-(-total // number_of), total * loads[0] // sum(loads)))
    least = 1 if total - largest >= number_of - 1 else 0
    given, spare = [largest] + [least] * (number_of - 1), total - largest - least * (number_of - 1)
    while spare > 0:
        candidates = [i for i in range(1, number_of) if given[i] < largest] or [i for i in range(1, number_of) if given[i] < bound]
        whole, remaining = sum([loads[i] for i in candidates]), spare
        for i in candidates:
            addition = min(bound - given[i], max(1, remaining * loads[i] // whole), spare)
            given[i] = given[i] + addition
            spare = spare - addition
    return np.array(given)


def bell_draw(key, extent, spread, reach, split=(), held_as=jnp.bfloat16):
    values = jax.random.normal(key, extent, jnp.float32) * spread
    if len(split) > 0:
        values = level_of(key, extent, split, -0.22, 0.18) * values
    return jnp.clip(values, min=-reach, max=reach).astype(held_as)


def setup_inputs(seed: int = 0, part: int = 0) -> dict:
    key_list = jax.random.split(jax.random.key(seed), 11)
    part_keys = jax.random.split(jax.random.fold_in(key_list[10], part), 11)
    row_x = bell_draw(part_keys[0], (ROWS, D), 1.0, 6.0, ((0, 64),))
    row_user_keys = jax.random.split(jax.random.fold_in(part_keys[1], 1), ROWS // ROWS_DEV)
    row_user_turns = jax.random.permutation(jax.random.fold_in(part_keys[1], 3), ROWS // ROWS_DEV)
    row_user = jax.vmap(lambda own, number: routed_block(jax.random.fold_in(part_keys[1], 2), own, number, ROWS_DEV, USERS, 1, CAP, 2))(row_user_keys, row_user_turns).reshape((ROWS, 1))
    user_owner = jax.random.permutation(part_keys[2], USERS).astype(jnp.int32)
    hist_len = ragged_sizes(part_keys[3], USERS, USERS * HIST // 2, HIST, 2).astype(jnp.int32)
    new_rows = bell_draw(part_keys[4], (USERS, NEW, D), 1.0, 6.0, ((0, 64),))
    cache_keys = bell_draw(part_keys[5], (USERS, HIST, D), 1.0, 6.0, ((0, 64),))
    cache_values = bell_draw(part_keys[6], (USERS, HIST, D), 1.0, 6.0, ((0, 64),))
    w_in = bell_draw(key_list[7], (D, 4 * D), D ** -0.5, 0.1875)
    w_out = bell_draw(key_list[8], (D, D), D ** -0.5, 0.1875)
    w_score = bell_draw(key_list[9], (D,), D ** -0.5, 0.1875, (), jnp.float32)
    return dict(row_x=row_x, row_user=row_user, user_owner=user_owner, hist_len=hist_len, new_rows=new_rows, cache_keys=cache_keys, cache_values=cache_values, w_in=w_in, w_out=w_out, w_score=w_score)


def layer_norm(v):
    mean = lax.optimization_barrier(jnp.mean(v, axis=-1, keepdims=True))
    cent = v - mean
    var = lax.optimization_barrier(jnp.mean(cent * cent, axis=-1, keepdims=True))
    return cent * lax.rsqrt(var + 1e-06)

def project(rows, weight):
    normed = layer_norm(rows.astype(jnp.float32)).astype(jnp.bfloat16)
    return jax.nn.silu(jnp.dot(normed, weight, preferred_element_type=jnp.float32)).astype(jnp.bfloat16)

def attend(query, keys, values, length, new_k, new_v, causal, counts):
    width = query.shape[1]
    heads = HEADS
    size = width // heads
    scale = 1.0 / size ** 0.5
    block = min(512, keys.shape[0])
    qh = query.astype(jnp.float32).reshape(query.shape[0], heads, size)

    def step(acc, b):
        start = (b * block).astype(jnp.int32)
        kb = lax.dynamic_slice_in_dim(keys, start, block, 0).astype(jnp.float32).reshape(block, heads, size)
        vb = lax.dynamic_slice_in_dim(values, start, block, 0).astype(jnp.float32).reshape(block, heads, size)
        s = jnp.einsum('rhd,khd->rhk', qh, kb) * scale
        valid = start + jnp.arange(block, dtype=jnp.int32) < length
        a = jnp.where(valid[None, None, :], jax.nn.silu(s), 0.0).astype(jnp.bfloat16)
        return (acc + jnp.einsum('rhk,khd->rhd', a.astype(jnp.float32), vb), None)
    acc = jnp.zeros((query.shape[0], heads, size), jnp.float32)
    acc, _ = lax.scan(step, acc, jnp.arange(keys.shape[0] // block, dtype=jnp.int32))
    nk = new_k.astype(jnp.float32).reshape(new_k.shape[0], heads, size)
    nv = new_v.astype(jnp.float32).reshape(new_v.shape[0], heads, size)
    s = jnp.einsum('rhd,khd->rhk', qh, nk) * scale
    a = jax.nn.silu(s)
    if causal:
        keep = jnp.arange(new_k.shape[0], dtype=jnp.int32)[None, :] <= jnp.arange(query.shape[0], dtype=jnp.int32)[:, None]
        a = jnp.where(keep[:, None, :], a, 0.0)
    a = a.astype(jnp.bfloat16)
    acc = acc + jnp.einsum('rhk,khd->rhd', a.astype(jnp.float32), nv)
    return (acc.reshape(query.shape[0], width) / counts[:, None]).astype(jnp.bfloat16)

def finish(rows, attention, gate, w_out):
    gated = (layer_norm(attention.astype(jnp.float32)) * gate.astype(jnp.float32)).astype(jnp.bfloat16)
    return rows.astype(jnp.float32) + jnp.dot(gated, w_out, preferred_element_type=jnp.float32)

def reference(row_x, row_user, user_owner, hist_len, new_rows, cache_keys, cache_values, w_in, w_out, w_score):
    width = row_x.shape[1]
    window = N_OWN * CAP
    owner_of_row = user_owner[row_user[:, 0]].astype(jnp.int32)
    order = jnp.argsort(owner_of_row, stable=True).astype(jnp.int32)
    counts = lax.optimization_barrier(jnp.sum((owner_of_row[:, None] == jnp.arange(USERS, dtype=jnp.int32)[None, :]).astype(jnp.int32), axis=0))
    starts = (jnp.cumsum(counts) - counts).astype(jnp.int32)
    order_pad = jnp.concatenate([order, jnp.zeros((window,), jnp.int32)])
    gate_all = project(row_x, w_in[:, 0:width])
    query_all = project(row_x, w_in[:, 2 * width:3 * width])

    def per_owner(scores, o):
        idx = lax.dynamic_slice_in_dim(order_pad, starts[o], window, 0)
        valid = jnp.arange(window, dtype=jnp.int32) < counts[o]
        length = hist_len[o]
        proj = project(new_rows[o], w_in)
        new_u = proj[:, 0:width]
        new_v = proj[:, width:2 * width]
        new_q = proj[:, 2 * width:3 * width]
        new_k = proj[:, 3 * width:]
        keys = cache_keys[o]
        values = cache_values[o]
        cand_n = jnp.full((window,), 1.0, jnp.float32) * (length + NEW).astype(jnp.float32)
        attention = attend(query_all[idx], keys, values, length, new_k, new_v, False, cand_n)
        out = finish(row_x[idx], attention, gate_all[idx], w_out)
        score = lax.optimization_barrier(jnp.sum(out * w_score[None, :], axis=1))
        target = jnp.where(valid, idx, ROWS).astype(jnp.int32)
        scores = scores.at[target].set(score, mode='drop')
        new_n = (length + 1 + jnp.arange(NEW, dtype=jnp.int32)).astype(jnp.float32)
        new_att = attend(new_q, keys, values, length, new_k, new_v, True, new_n)
        new_out = finish(new_rows[o], new_att, new_u, w_out).astype(jnp.bfloat16)
        return (scores, new_out)
    scores, new_out = lax.scan(per_owner, jnp.zeros((ROWS,), jnp.float32), jnp.arange(USERS, dtype=jnp.int32))
    return (scores, new_out)
```

```python
import jax
import jax.numpy as jnp
from jax import lax
from jax.experimental import pallas as pl
from jax.experimental.pallas import tpu as pltpu
from jax.sharding import PartitionSpec as P

HEADS = 8
NEW = 64
BF = jnp.bfloat16
F32 = jnp.float32
VMEM_LIMIT = 56 * 1024 * 1024


def dot(a, b, dims=((1,), (0,))):
    return lax.dot_general(a, b, (dims, ((), ())), preferred_element_type=F32)


def normalize(v):
    mean = jnp.mean(v, axis=-1, keepdims=True)
    cent = v - mean
    var = jnp.mean(cent * cent, axis=-1, keepdims=True)
    return cent * lax.rsqrt(var + 1e-06)


def silu(v):
    half = 0.5 * v
    return half + half * jnp.tanh(half)


def split3(v):
    hi = v.astype(BF)
    rest = v - hi.astype(F32)
    mid = rest.astype(BF)
    low = (rest - mid.astype(F32)).astype(BF)
    return hi, mid, low


def split_rows(row):
    width = row.shape[1]
    hi, mid, low = split3(row)
    place = lax.broadcasted_iota(jnp.int32, (8, width), 0)
    parts = jnp.where(place == 0, hi.astype(F32), 0.0)
    parts = jnp.where(place == 1, mid.astype(F32), parts)
    return jnp.where(place == 2, low.astype(F32), parts).astype(BF)


def fill(out_ref, slots, first, owner, position, normed_ref):
    rows = normed_ref.shape[0]
    inside = jnp.logical_and(position >= first, position < first + slots)
    key = jnp.where(inside, owner * slots + position - first, -1)
    step = 256
    for b in range(out_ref.shape[0] // step):
        at = lax.broadcasted_iota(jnp.int32, (step, rows), 0) + b * step
        pick = jnp.where(at == key, 1.0, 0.0).astype(BF)
        out_ref[b * step : (b + 1) * step, :] = dot(pick, normed_ref[...]).astype(BF)


def route_kernel(
    slots, x_ref, user_ref, owner_ref, score_ref, buf_ref, normed_ref, place_ref, base_ref
):
    rows, width = x_ref.shape
    users = owner_ref.shape[1]
    step = 128
    for b in range(rows // step):
        part = slice(b * step, (b + 1) * step)
        normed_ref[part, :] = normalize(x_ref[part, :].astype(F32)).astype(BF)
    along = lax.broadcasted_iota(jnp.int32, (users, users), 0)
    across = lax.broadcasted_iota(jnp.int32, (users, users), 1)
    owners = jnp.sum(
        jnp.where(along == across, owner_ref[...], 0).astype(F32), axis=1, keepdims=True
    )
    before = lax.broadcasted_iota(jnp.int32, (step, step), 0) < lax.broadcasted_iota(
        jnp.int32, (step, step), 1
    )
    before = jnp.where(before, 1.0, 0.0).astype(BF)
    seen = jnp.zeros((users, 1), F32)
    for b in range(rows // step):
        part = slice(b * step, (b + 1) * step)
        match = lax.broadcasted_iota(jnp.int32, (users, step), 0) == user_ref[:, part]
        match = jnp.where(match, 1.0, 0.0)
        earlier = dot(match.astype(BF), before) + seen
        seen = seen + jnp.sum(match, axis=1, keepdims=True)
        position = jnp.sum(earlier * match, axis=0, keepdims=True)
        owner = jnp.sum(owners * match, axis=0, keepdims=True)
        place_ref[0:1, part] = owner.astype(jnp.int32)
        place_ref[1:2, part] = position.astype(jnp.int32)
    base = dot(split_rows(score_ref[...]), x_ref[...], ((1,), (1,)))
    base_ref[...] = jnp.sum(base, axis=0, keepdims=True)
    fill(buf_ref, slots, 0, place_ref[0:1, :], place_ref[1:2, :], normed_ref)


def fill_kernel(slots, first, place_ref, normed_ref, buf_ref):
    fill(buf_ref, slots, first, place_ref[0:1, :], place_ref[1:2, :], normed_ref)


def new_kernel(
    length_ref, new_ref, w_in_ref, keys_ref, values_ref, w_out_ref, score_ref,
    k_ref, v_ref, vec_ref, out_ref,
):
    length = length_ref[0]
    fresh, width = new_ref.shape
    hist = keys_ref.shape[0]
    size = width // HEADS
    rows = new_ref[...].astype(F32)
    normed = normalize(rows).astype(BF)
    cut = [
        silu(dot(normed, w_in_ref[:, i * width : (i + 1) * width])).astype(BF) for i in range(4)
    ]
    gate, value, query, key = cut
    k_ref[0:hist, :] = keys_ref[...]
    k_ref[hist : hist + fresh, :] = key
    for b in range(0, hist, 128):
        at = lax.broadcasted_iota(jnp.int32, (128, width), 0) + b
        kept = jnp.where(at < length, values_ref[b : b + 128, :].astype(F32), 0.0)
        v_ref[b : b + 128, :] = kept.astype(BF)
    v_ref[hist : hist + fresh, :] = value
    vec = jnp.sum(dot(split_rows(score_ref[...]), w_out_ref[...], ((1,), (1,))), axis=0, keepdims=True)
    vec_ref[...] = split_rows(vec)
    total = hist + fresh
    at = lax.broadcasted_iota(jnp.int32, (fresh, total), 1)
    line = lax.broadcasted_iota(jnp.int32, (fresh, total), 0)
    keep = at <= line + hist
    outs = []
    for h in range(HEADS):
        cols = slice(h * size, (h + 1) * size)
        s = dot(query[:, cols], k_ref[:, cols], ((1,), (1,))) * (1.0 / size**0.5)
        a = jnp.where(keep, silu(s), 0.0).astype(BF)
        outs.append(dot(a, v_ref[:, cols]))
    number = lax.broadcasted_iota(jnp.int32, (fresh, 1), 0) + (length + 1)
    att = (jnp.concatenate(outs, axis=1) / number.astype(F32)).astype(BF)
    gated = (normalize(att.astype(F32)) * gate.astype(F32)).astype(BF)
    out_ref[...] = (rows + dot(gated, w_out_ref[...])).astype(BF)


def rank_kernel(slots, first, length_ref, x_ref, wq_ref, wu_ref, k_ref, v_ref, vec_ref, out_ref):
    count, width = x_ref.shape
    size = width // HEADS
    x = x_ref[...]
    query = (silu(dot(x, wq_ref[...])) * (0.5 / size**0.5)).astype(BF)
    outs = []
    for h in range(HEADS):
        cols = slice(h * size, (h + 1) * size)
        s = dot(query[:, cols], k_ref[:, cols], ((1,), (1,)))
        a = (s + s * jnp.tanh(s)).astype(BF)
        outs.append(dot(a, v_ref[:, cols]))
    number = (length_ref[0] + NEW).astype(F32)
    att = (jnp.concatenate(outs, axis=1) / number).astype(BF)
    gate = silu(dot(x, wu_ref[...])).astype(BF)
    gated = (normalize(att.astype(F32)) * gate.astype(F32)).astype(BF)
    line = jnp.sum(dot(vec_ref[...], gated, ((1,), (1,))), axis=0, keepdims=True)
    groups = count // slots
    at = lax.broadcasted_iota(jnp.int32, (groups, count), 1)
    group = lax.broadcasted_iota(jnp.int32, (groups, count), 0)
    mine = jnp.logical_and(at >= group * slots, at < (group + 1) * slots)
    row = lax.broadcasted_iota(jnp.int32, (count, 128), 0)
    lane = lax.broadcasted_iota(jnp.int32, (count, 128), 1)
    spread = jnp.where(lax.rem(row, slots) + first == lane, 1.0, 0.0).astype(BF)
    total = jnp.zeros((groups, 128), F32)
    for part in split3(line):
        total += dot(jnp.where(mine, part.astype(F32), 0.0).astype(BF), spread)
    out_ref[...] = total


def score_kernel(place_ref, base_ref, ret_ref, out_ref):
    parties, lanes = ret_ref.shape
    rows = base_ref.shape[1]
    owner = place_ref[0:1, :]
    position = place_ref[1:2, :]
    match = lax.broadcasted_iota(jnp.int32, (parties, rows), 0) == owner
    match = jnp.where(match, 1.0, 0.0).astype(BF)
    got = jnp.zeros((lanes, rows), F32)
    for part in split3(ret_ref[...]):
        got += dot(part, match, ((0,), (0,)))
    slot = lax.broadcasted_iota(jnp.int32, (lanes, rows), 0) == position
    out_ref[...] = base_ref[...] + jnp.sum(jnp.where(slot, got, 0.0), axis=0, keepdims=True)


def whole(n):
    return [pl.BlockSpec(memory_space=pltpu.VMEM)] * n


def params():
    return pltpu.CompilerParams(vmem_limit_bytes=VMEM_LIMIT)


def cost(macs, moved, transcendentals=0):
    return pl.CostEstimate(flops=2 * macs, bytes_accessed=moved, transcendentals=transcendentals)


def on_device(
    row_x, row_user, user_owner, hist_len, new_rows, cache_keys, cache_values, w_in, w_out, w_score
):
    n_own = lax.axis_size("own")
    rows, width = row_x.shape
    users = user_owner.shape[0]
    hist = cache_keys.shape[1]
    total = hist + NEW
    capacity = 2 * rows // n_own
    chunks = (capacity // 2, capacity // 2)
    score_row = w_score.reshape(1, width)
    sds = jax.ShapeDtypeStruct

    def all_to_all(v):
        return lax.all_to_all(v, "own", split_axis=0, concat_axis=0, tiled=True)

    buf, normed, place, base = pl.pallas_call(
        lambda *refs: route_kernel(chunks[0], *refs),
        out_shape=(
            sds((n_own * chunks[0], width), BF),
            sds((rows, width), BF),
            sds((2, rows), jnp.int32),
            sds((1, rows), F32),
        ),
        in_specs=whole(4),
        out_specs=tuple(whole(4)),
        compiler_params=params(),
        cost_estimate=cost(rows * width * n_own * chunks[0], 3 * 2 * rows * width),
        name="route",
    )(row_x, row_user.reshape(1, rows), user_owner.reshape(1, users), score_row)

    pieces = [all_to_all(buf.reshape(n_own, chunks[0], width))]
    first = chunks[0]
    for slots in chunks[1:]:
        buf = pl.pallas_call(
            lambda *refs, slots=slots, first=first: fill_kernel(slots, first, *refs),
            out_shape=sds((n_own * slots, width), BF),
            in_specs=whole(2),
            out_specs=whole(1)[0],
            compiler_params=params(),
            cost_estimate=cost(rows * width * n_own * slots, 2 * 2 * rows * width),
            name="fill",
        )(place, normed)
        pieces.append(all_to_all(buf.reshape(n_own, slots, width)))
        first += slots

    keys, values, vec, new_out = pl.pallas_call(
        new_kernel,
        out_shape=(
            sds((total, width), BF),
            sds((total, width), BF),
            sds((8, width), BF),
            sds((NEW, width), BF),
        ),
        in_specs=[pl.BlockSpec(memory_space=pltpu.SMEM)] + whole(6),
        out_specs=tuple(whole(4)),
        compiler_params=params(),
        cost_estimate=cost(8 * NEW * width * width, 20 * width * width),
        name="fresh",
    )(hist_len, new_rows[0], w_in, cache_keys[0], cache_values[0], w_out, score_row)

    tile = 256
    result = None
    first = 0
    for piece, slots in zip(pieces, chunks):
        count = n_own * slots
        part = pl.pallas_call(
            lambda *refs, slots=slots, first=first: rank_kernel(slots, first, *refs),
            grid=(count // tile,),
            out_shape=sds((n_own, 128), F32),
            in_specs=[
                pl.BlockSpec(memory_space=pltpu.SMEM),
                pl.BlockSpec((tile, width), lambda i: (i, 0)),
                pl.BlockSpec((width, width), lambda i: (0, 2)),
                pl.BlockSpec((width, width), lambda i: (0, 0)),
                pl.BlockSpec((total, width), lambda i: (0, 0)),
                pl.BlockSpec((total, width), lambda i: (0, 0)),
                pl.BlockSpec((8, width), lambda i: (0, 0)),
            ],
            out_specs=pl.BlockSpec((tile // slots, 128), lambda i: (i, 0)),
            compiler_params=params(),
            cost_estimate=cost(
                count * width * (2 * width + 4 * total), 10 * width * width, count * HEADS * total
            ),
            name="rank",
        )(hist_len, piece.reshape(count, width), w_in, w_in, keys, values, vec)
        result = part if result is None else result + part
        first += slots

    returned = all_to_all(result.reshape(n_own, 1, 128)).reshape(n_own, 128)
    scores = pl.pallas_call(
        score_kernel,
        out_shape=sds((1, rows), F32),
        in_specs=whole(3),
        out_specs=whole(1)[0],
        compiler_params=params(),
        name="scores",
    )(place, base, returned)
    return (scores.reshape(rows), new_out[None])


def solution(mesh):
    placed = (
        P(("grp", "own"), None),
        P(("grp", "own"), None),
        P("grp"),
        P(("grp", "own")),
        P(("grp", "own"), None, None),
        P(("grp", "own"), None, None),
        P(("grp", "own"), None, None),
        P(),
        P(),
        P(),
    )
    return jax.shard_map(
        on_device,
        mesh=mesh,
        in_specs=placed,
        out_specs=(P(("grp", "own")), P(("grp", "own"), None, None)),
        check_vma=False,
    )
```

```python
import jax
import jax.numpy as jnp
from jax import lax
from jax.experimental import pallas as pl
from jax.experimental.pallas import tpu as pltpu
from jax.sharding import PartitionSpec as P

HEADS = 8
NEW = 64
BF = jnp.bfloat16
F32 = jnp.float32
VMEM_LIMIT = 56 * 1024 * 1024
SLOTS = 16
TILE = 512


def dot(a, b, dims=((1,), (0,))):
    return lax.dot_general(a, b, (dims, ((), ())), preferred_element_type=F32)


def normalize(v):
    mean = jnp.mean(v, axis=-1, keepdims=True)
    cent = v - mean
    var = jnp.mean(cent * cent, axis=-1, keepdims=True)
    return cent * lax.rsqrt(var + 1e-06)


def silu(v):
    half = 0.5 * v
    return half + half * jnp.tanh(half)


def split3(v):
    hi = v.astype(BF)
    rest = v - hi.astype(F32)
    mid = rest.astype(BF)
    low = (rest - mid.astype(F32)).astype(BF)
    return hi, mid, low


def split_rows(row):
    width = row.shape[1]
    hi, mid, low = split3(row)
    place = lax.broadcasted_iota(jnp.int32, (8, width), 0)
    parts = jnp.where(place == 0, hi.astype(F32), 0.0)
    parts = jnp.where(place == 1, mid.astype(F32), parts)
    return jnp.where(place == 2, low.astype(F32), parts).astype(BF)


def place_rows(user_ref, owner_ref, place_ref):
    rows = user_ref.shape[1]
    users = owner_ref.shape[1]
    step = 128
    along = lax.broadcasted_iota(jnp.int32, (users, users), 0)
    across = lax.broadcasted_iota(jnp.int32, (users, users), 1)
    owners = jnp.sum(
        jnp.where(along == across, owner_ref[...], 0).astype(F32), axis=1, keepdims=True
    )
    before = lax.broadcasted_iota(jnp.int32, (step, step), 0) < lax.broadcasted_iota(
        jnp.int32, (step, step), 1
    )
    before = jnp.where(before, 1.0, 0.0).astype(BF)
    seen = jnp.zeros((users, 1), F32)
    for b in range(rows // step):
        part = slice(b * step, (b + 1) * step)
        match = lax.broadcasted_iota(jnp.int32, (users, step), 0) == user_ref[:, part]
        match = jnp.where(match, 1.0, 0.0)
        earlier = dot(match.astype(BF), before) + seen
        seen = seen + jnp.sum(match, axis=1, keepdims=True)
        position = jnp.sum(earlier * match, axis=0, keepdims=True)
        owner = jnp.sum(owners * match, axis=0, keepdims=True)
        place_ref[0:1, part] = owner.astype(jnp.int32)
        place_ref[1:2, part] = position.astype(jnp.int32)


def fill(out_ref, slots, first, place_ref, normed_ref, done=None):
    rows = normed_ref.shape[0]
    owner = place_ref[0:1, :]
    position = place_ref[1:2, :]
    inside = jnp.logical_and(position >= first, position < first + slots)
    key = jnp.where(inside, owner * slots + position - first, -1)
    step = 256
    for b in range(out_ref.shape[0] // step):
        at = lax.broadcasted_iota(jnp.int32, (step, rows), 0) + b * step
        pick = jnp.where(at == key, 1.0, 0.0).astype(BF)
        out_ref[b * step : (b + 1) * step, :] = dot(pick, normed_ref[...]).astype(BF)
        if done is not None:
            done(b, slice(b * step, (b + 1) * step))


def route_kernel(
    slots, x_hbm, user_ref, owner_ref, buf_hbm, place_ref, x_ref, normed_ref, buf_ref, sem_in, sem_out
):
    rows = x_ref.shape[0]
    step = rows // 4
    cuts = [slice(b * step, (b + 1) * step) for b in range(4)]
    loads = [
        pltpu.make_async_copy(x_hbm.at[cut, :], x_ref.at[cut, :], sem_in.at[b])
        for b, cut in enumerate(cuts)
    ]
    for load in loads:
        load.start()
    place_rows(user_ref, owner_ref, place_ref)
    for load, cut in zip(loads, cuts):
        load.wait()
        normed_ref[cut, :] = normalize(x_ref[cut, :].astype(F32)).astype(BF)
    stores = []

    def send(b, cut):
        store = pltpu.make_async_copy(buf_ref.at[cut, :], buf_hbm.at[cut, :], sem_out.at[b])
        store.start()
        stores.append(store)

    fill(buf_ref, slots, 0, place_ref, normed_ref, send)
    for store in stores:
        store.wait()


def fill_second(slots, first, x_ref, place_ref, score_ref, buf_ref, base_ref, normed_ref):
    rows = x_ref.shape[0]
    step = 128
    for b in range(rows // step):
        part = slice(b * step, (b + 1) * step)
        normed_ref[part, :] = normalize(x_ref[part, :].astype(F32)).astype(BF)
    base = dot(split_rows(score_ref[...]), x_ref[...], ((1,), (1,)))
    base_ref[...] = jnp.sum(base, axis=0, keepdims=True)
    fill(buf_ref, slots, first, place_ref, normed_ref)


def flip(v):
    return jnp.transpose(v.astype(F32)).astype(BF)


def new_kernel(
    slots, length_ref, new_ref, w_in_ref, keys_ref, values_ref, w_out_ref, score_ref, x_ref, place_ref,
    k_ref, v_ref, wq_ref, wu_ref, vec_ref, out_ref, buf_ref, base_ref, normed_ref,
):
    fill_second(slots, slots, x_ref, place_ref, score_ref, buf_ref, base_ref, normed_ref)
    length = length_ref[0]
    fresh, width = new_ref.shape
    hist = keys_ref.shape[0]
    size = width // HEADS
    step = 256
    rows = new_ref[...].astype(F32)
    normed = normalize(rows).astype(BF)
    cut = [
        silu(dot(normed, w_in_ref[:, i * width : (i + 1) * width])).astype(BF) for i in range(4)
    ]
    gate, value, query, key = cut
    k_ref[0:hist, :] = keys_ref[...]
    k_ref[hist : hist + fresh, :] = key
    for i in range(0, hist, step):
        kept = lax.broadcasted_iota(jnp.int32, (step, step), 0) + i < length
        for j in range(0, width, step):
            block = values_ref[i : i + step, j : j + step].astype(F32)
            v_ref[j : j + step, i : i + step] = flip(jnp.where(kept, block, 0.0))
    v_ref[:, hist : hist + fresh] = flip(value)
    for i in range(0, width, step):
        for j in range(0, width, step):
            wu_ref[j : j + step, i : i + step] = flip(w_in_ref[i : i + step, j : j + step])
            wq_ref[j : j + step, i : i + step] = flip(
                w_in_ref[i : i + step, 2 * width + j : 2 * width + j + step]
            )
    vec = jnp.sum(dot(split_rows(score_ref[...]), w_out_ref[...], ((1,), (1,))), axis=0, keepdims=True)
    vec_ref[...] = split_rows(vec)
    total = hist + fresh
    at = lax.broadcasted_iota(jnp.int32, (fresh, total), 1)
    line = lax.broadcasted_iota(jnp.int32, (fresh, total), 0)
    keep = at <= line + hist
    outs = []
    for h in range(HEADS):
        cols = slice(h * size, (h + 1) * size)
        s = dot(query[:, cols], k_ref[:, cols], ((1,), (1,))) * (1.0 / size**0.5)
        a = jnp.where(keep, silu(s), 0.0).astype(BF)
        outs.append(dot(a, v_ref[cols, :], ((1,), (1,))))
    number = lax.broadcasted_iota(jnp.int32, (fresh, 1), 0) + (length + 1)
    att = (jnp.concatenate(outs, axis=1) / number.astype(F32)).astype(BF)
    gated = (normalize(att.astype(F32)) * gate.astype(F32)).astype(BF)
    out_ref[...] = (rows + dot(gated, w_out_ref[...])).astype(BF)


def rank_lines(share, x, wq, wu, k, v, vec, need):
    width = x.shape[1]
    size = width // HEADS
    need("wq")
    query = (silu(dot(wq[...], x, ((1,), (1,)))) * (0.5 / size**0.5)).astype(BF)
    outs = []
    need("k")
    for h in range(HEADS):
        cols = slice(h * size, (h + 1) * size)
        s = dot(k[:, cols], query[cols, :])
        a = (s + s * jnp.tanh(s)).astype(BF)
        need("v")
        outs.append(dot(v[cols, :], a))
    att = (jnp.concatenate(outs, axis=0) * share).astype(BF).astype(F32)
    need("wu")
    gate = silu(dot(wu[...], x, ((1,), (1,)))).astype(BF)
    mean = jnp.mean(att, axis=0, keepdims=True)
    cent = att - mean
    var = jnp.mean(cent * cent, axis=0, keepdims=True)
    gated = (cent * lax.rsqrt(var + 1e-06) * gate.astype(F32)).astype(BF)
    return jnp.sum(dot(vec[...], gated), axis=0, keepdims=True)


def rank_kernel(last, *refs):
    if last:
        length_ref, x, vec_ref, prev_ref, wq_hbm, wu_hbm, k_hbm, v_hbm, out_ref = refs[:9]
    else:
        length_ref, x, vec_ref, wq_hbm, wu_hbm, k_hbm, v_hbm, out_ref = refs[:8]
    wq, wu, k, v, sem = refs[-5:]
    left = {}
    for i, (name, a, b) in enumerate(
        (("wq", wq_hbm, wq), ("k", k_hbm, k), ("v", v_hbm, v), ("wu", wu_hbm, wu))
    ):
        left[name] = pltpu.make_async_copy(a, b, sem.at[i])
        left[name].start()

    def need(name):
        if name in left:
            left.pop(name).wait()

    share = 1.0 / (length_ref[0] + NEW).astype(F32)
    for i in range(x.shape[0] // TILE):
        c = slice(i * TILE, (i + 1) * TILE)
        line = rank_lines(share, x[c, :], wq, wu, k, v, vec_ref, need)
        if not last:
            out_ref[:, c] = line
            continue
        odd = lax.rem(lax.broadcasted_iota(jnp.int32, (16, 128), 0), 2) == 1
        for j in range(TILE // 128):
            b = i * (TILE // 128) + j
            mine = line[:, j * 128 : (j + 1) * 128]
            early = prev_ref[:, b * 128 : (b + 1) * 128]
            out_ref[16 * b : 16 * (b + 1), :] = jnp.where(odd, mine, early)


def score_kernel(me_ref, place_ref, base_ref, ret_ref, out_ref):
    parties = ret_ref.shape[0] // 2
    rows = base_ref.shape[1]
    owner = place_ref[0:1, :]
    position = place_ref[1:2, :]
    half = position >= SLOTS
    at = 2 * owner + half.astype(jnp.int32)
    match = lax.broadcasted_iota(jnp.int32, (2 * parties, rows), 0) == at
    match = jnp.where(match, 1.0, 0.0).astype(BF)
    got = jnp.zeros((128, rows), F32)
    for part in split3(ret_ref[...]):
        got += dot(part, match, ((0,), (0,)))
    lane = position - jnp.where(half, SLOTS, 0) + lax.rem(me_ref[0], 128 // SLOTS) * SLOTS
    slot = lax.broadcasted_iota(jnp.int32, (128, rows), 0) == lane
    out_ref[...] = base_ref[...] + jnp.sum(jnp.where(slot, got, 0.0), axis=0, keepdims=True)


def whole(n):
    return [pl.BlockSpec(memory_space=pltpu.VMEM)] * n


def far(n):
    return [pl.BlockSpec(memory_space=pl.ANY)] * n


def small(n):
    return [pl.BlockSpec(memory_space=pltpu.SMEM)] * n


def params():
    return pltpu.CompilerParams(vmem_limit_bytes=VMEM_LIMIT)


def cost(macs, moved, transcendentals=0):
    return pl.CostEstimate(flops=2 * macs, bytes_accessed=moved, transcendentals=transcendentals)


def on_device(
    row_x, row_user, user_owner, hist_len, new_rows, cache_keys, cache_values, w_in, w_out, w_score
):
    n_own = lax.axis_size("own")
    rows, width = row_x.shape
    users = user_owner.shape[0]
    hist = cache_keys.shape[1]
    total = hist + NEW
    count = n_own * SLOTS
    score_row = w_score.reshape(1, width)
    sds = jax.ShapeDtypeStruct
    dma = pltpu.SemaphoreType.DMA

    def all_to_all(v):
        return lax.all_to_all(v, "own", split_axis=0, concat_axis=0, tiled=True)

    buf, place = pl.pallas_call(
        lambda *refs: route_kernel(SLOTS, *refs),
        out_shape=(sds((count, width), BF), sds((2, rows), jnp.int32)),
        in_specs=far(1) + whole(2),
        out_specs=(far(1)[0], whole(1)[0]),
        scratch_shapes=[
            pltpu.VMEM((rows, width), BF),
            pltpu.VMEM((rows, width), BF),
            pltpu.VMEM((count, width), BF),
            dma((4,)),
            dma((count // 256,)),
        ],
        compiler_params=params(),
        cost_estimate=cost(rows * width * count, 2 * 2 * rows * width),
        name="route",
    )(row_x, row_user.reshape(1, rows), user_owner.reshape(1, users))
    piece0 = all_to_all(buf.reshape(n_own, SLOTS, width)).reshape(count, width)

    keys, values, wq, wu, vec, new_out, buf, base = pl.pallas_call(
        lambda *refs: new_kernel(SLOTS, *refs),
        out_shape=(
            sds((total, width), BF),
            sds((width, total), BF),
            sds((width, width), BF),
            sds((width, width), BF),
            sds((8, width), BF),
            sds((NEW, width), BF),
            sds((count, width), BF),
            sds((1, rows), F32),
        ),
        in_specs=small(1) + whole(8),
        out_specs=tuple(whole(8)),
        scratch_shapes=[pltpu.VMEM((rows, width), BF)],
        compiler_params=params(),
        cost_estimate=cost(8 * NEW * width * width + rows * width * count, 24 * width * width),
        name="fresh",
    )(hist_len, new_rows[0], w_in, cache_keys[0], cache_values[0], w_out, score_row, row_x, place)
    piece1 = all_to_all(buf.reshape(n_own, SLOTS, width)).reshape(count, width)

    def rank(piece, prev):
        last = prev is not None
        return pl.pallas_call(
            lambda *refs: rank_kernel(last, *refs),
            out_shape=sds((2 * n_own, 128), F32) if last else sds((1, count), F32),
            in_specs=small(1) + whole(3 if last else 2) + far(4),
            out_specs=whole(1)[0],
            scratch_shapes=[
                pltpu.VMEM((width, width), BF),
                pltpu.VMEM((width, width), BF),
                pltpu.VMEM((total, width), BF),
                pltpu.VMEM((width, total), BF),
                dma((4,)),
            ],
            compiler_params=params(),
            cost_estimate=cost(
                count * width * (2 * width + 4 * total), 10 * width * width, count * HEADS * total
            ),
            name="rank",
        )(hist_len, piece, vec, *([prev] if last else []), wq, wu, keys, values)

    result = rank(piece1, rank(piece0, None))
    returned = all_to_all(result.reshape(n_own, 2, 128)).reshape(2 * n_own, 128)
    scores = pl.pallas_call(
        score_kernel,
        out_shape=sds((1, rows), F32),
        in_specs=small(1) + whole(3),
        out_specs=whole(1)[0],
        compiler_params=params(),
        name="scores",
    )(lax.axis_index("own").reshape(1), place, base, returned)
    return (scores.reshape(rows), new_out[None])


def solution(mesh):
    placed = (
        P(("grp", "own"), None),
        P(("grp", "own"), None),
        P("grp"),
        P(("grp", "own")),
        P(("grp", "own"), None, None),
        P(("grp", "own"), None, None),
        P(("grp", "own"), None, None),
        P(),
        P(),
        P(),
    )
    return jax.shard_map(
        on_device,
        mesh=mesh,
        in_specs=placed,
        out_specs=(P(("grp", "own")), P(("grp", "own"), None, None)),
        check_vma=False,
    )
```

```python
import jax
import jax.numpy as jnp
from jax import lax
from jax.experimental import pallas as pl
from jax.experimental.pallas import tpu as pltpu
from jax.sharding import PartitionSpec as P

HEADS = 8
NEW = 64
BF = jnp.bfloat16
F32 = jnp.float32
VMEM_LIMIT = 56 * 1024 * 1024
SLOTS = 16
TILE = 512


def dot(a, b, dims=((1,), (0,))):
    return lax.dot_general(a, b, (dims, ((), ())), preferred_element_type=F32)


def normalize(v):
    mean = jnp.mean(v, axis=-1, keepdims=True)
    cent = v - mean
    var = jnp.mean(cent * cent, axis=-1, keepdims=True)
    return cent * lax.rsqrt(var + 1e-06)


def silu(v):
    half = 0.5 * v
    return half + half * jnp.tanh(half)


def split3(v):
    hi = v.astype(BF)
    rest = v - hi.astype(F32)
    mid = rest.astype(BF)
    low = (rest - mid.astype(F32)).astype(BF)
    return hi, mid, low


def split_rows(row):
    width = row.shape[1]
    hi, mid, low = split3(row)
    place = lax.broadcasted_iota(jnp.int32, (8, width), 0)
    parts = jnp.where(place == 0, hi.astype(F32), 0.0)
    parts = jnp.where(place == 1, mid.astype(F32), parts)
    return jnp.where(place == 2, low.astype(F32), parts).astype(BF)


def place_rows(user_ref, owner_ref, place_ref):
    rows = user_ref.shape[1]
    users = owner_ref.shape[1]
    step = 128
    along = lax.broadcasted_iota(jnp.int32, (users, users), 0)
    across = lax.broadcasted_iota(jnp.int32, (users, users), 1)
    owners = jnp.sum(
        jnp.where(along == across, owner_ref[...], 0).astype(F32), axis=1, keepdims=True
    )
    before = lax.broadcasted_iota(jnp.int32, (step, step), 0) < lax.broadcasted_iota(
        jnp.int32, (step, step), 1
    )
    before = jnp.where(before, 1.0, 0.0).astype(BF)
    seen = jnp.zeros((users, 1), F32)
    for b in range(rows // step):
        part = slice(b * step, (b + 1) * step)
        match = lax.broadcasted_iota(jnp.int32, (users, step), 0) == user_ref[:, part]
        match = jnp.where(match, 1.0, 0.0)
        earlier = dot(match.astype(BF), before) + seen
        seen = seen + jnp.sum(match, axis=1, keepdims=True)
        position = jnp.sum(earlier * match, axis=0, keepdims=True)
        owner = jnp.sum(owners * match, axis=0, keepdims=True)
        place_ref[0:1, part] = owner.astype(jnp.int32)
        place_ref[1:2, part] = position.astype(jnp.int32)


def fill(out_ref, slots, first, place_ref, normed_ref, done=None):
    rows = normed_ref.shape[0]
    owner = place_ref[0:1, :]
    position = place_ref[1:2, :]
    inside = jnp.logical_and(position >= first, position < first + slots)
    key = jnp.where(inside, owner * slots + position - first, -1)
    step = 256
    for b in range(out_ref.shape[0] // step):
        at = lax.broadcasted_iota(jnp.int32, (step, rows), 0) + b * step
        pick = jnp.where(at == key, 1.0, 0.0).astype(BF)
        out_ref[b * step : (b + 1) * step, :] = dot(pick, normed_ref[...]).astype(BF)
        if done is not None:
            done(b, slice(b * step, (b + 1) * step))


def route_kernel(
    slots, x_hbm, user_ref, owner_ref, buf_hbm, place_ref, x_ref, buf_ref, sem_in, sem_out
):
    load = pltpu.make_async_copy(x_hbm, x_ref, sem_in)
    load.start()
    place_rows(user_ref, owner_ref, place_ref)
    load.wait()
    stores = []

    def send(b, cut):
        store = pltpu.make_async_copy(buf_ref.at[cut, :], buf_hbm.at[cut, :], sem_out.at[b])
        store.start()
        stores.append(store)

    fill(buf_ref, slots, 0, place_ref, x_ref, send)
    for store in stores:
        store.wait()


def fill_second(slots, first, x_ref, place_ref, score_ref, buf_ref, base_ref, normed_ref):
    rows = x_ref.shape[0]
    step = 128
    for b in range(rows // step):
        part = slice(b * step, (b + 1) * step)
        normed_ref[part, :] = normalize(x_ref[part, :].astype(F32)).astype(BF)
    base = dot(split_rows(score_ref[...]), x_ref[...], ((1,), (1,)))
    base_ref[...] = jnp.sum(base, axis=0, keepdims=True)
    fill(buf_ref, slots, first, place_ref, normed_ref)


def flip(v, scale=1.0):
    return jnp.transpose(v.astype(F32) * scale).astype(BF)


def new_kernel(
    slots, length_ref, new_ref, w_in_ref, keys_ref, values_ref, w_out_ref, score_ref, x_ref, place_ref,
    k_ref, v_ref, wq_ref, wu_ref, vec_ref, out_ref, buf_ref, base_ref, normed_ref,
):
    fill_second(slots, slots, x_ref, place_ref, score_ref, buf_ref, base_ref, normed_ref)
    length = length_ref[0]
    fresh, width = new_ref.shape
    hist = keys_ref.shape[0]
    size = width // HEADS
    step = 256
    rows = new_ref[...].astype(F32)
    normed = normalize(rows).astype(BF)
    cut = [
        silu(dot(normed, w_in_ref[:, i * width : (i + 1) * width])).astype(BF) for i in range(4)
    ]
    gate, value, query, key = cut
    k_ref[0:hist, :] = keys_ref[...]
    k_ref[hist : hist + fresh, :] = key
    for i in range(0, hist, step):
        kept = lax.broadcasted_iota(jnp.int32, (step, step), 0) + i < length
        for j in range(0, width, step):
            block = values_ref[i : i + step, j : j + step].astype(F32)
            v_ref[j : j + step, i : i + step] = flip(jnp.where(kept, block, 0.0))
    v_ref[:, hist : hist + fresh] = flip(value)
    for i in range(0, width, step):
        for j in range(0, width, step):
            wu_ref[j : j + step, i : i + step] = flip(w_in_ref[i : i + step, j : j + step], 0.5)
            wq_ref[j : j + step, i : i + step] = flip(
                w_in_ref[i : i + step, 2 * width + j : 2 * width + j + step], 0.5
            )
    vec = jnp.sum(dot(split_rows(score_ref[...]), w_out_ref[...], ((1,), (1,))), axis=0, keepdims=True)
    vec_ref[...] = split_rows(vec)
    total = hist + fresh
    at = lax.broadcasted_iota(jnp.int32, (fresh, total), 1)
    line = lax.broadcasted_iota(jnp.int32, (fresh, total), 0)
    keep = at <= line + hist
    outs = []
    for h in range(HEADS):
        cols = slice(h * size, (h + 1) * size)
        s = dot(query[:, cols], k_ref[:, cols], ((1,), (1,))) * (1.0 / size**0.5)
        a = jnp.where(keep, silu(s), 0.0).astype(BF)
        outs.append(dot(a, v_ref[cols, :], ((1,), (1,))))
    number = lax.broadcasted_iota(jnp.int32, (fresh, 1), 0) + (length + 1)
    att = (jnp.concatenate(outs, axis=1) / number.astype(F32)).astype(BF)
    gated = (normalize(att.astype(F32)) * gate.astype(F32)).astype(BF)
    out_ref[...] = (rows + dot(gated, w_out_ref[...])).astype(BF)


def rank_lines(share, x, wq, wu, k, v, vec, need):
    width = x.shape[1]
    size = width // HEADS
    step = 256

    def act(half):
        return half + half * jnp.tanh(half)

    def project(w, scale):
        parts = [dot(w[i : i + step, :], x, ((1,), (1,))) for i in range(0, width, step)]
        return jnp.concatenate([(act(p) * scale).astype(BF) for p in parts], axis=0)

    need("wq")
    query = project(wq, 0.5 / size**0.5)
    outs = []
    need("k")
    for h in range(HEADS):
        cols = slice(h * size, (h + 1) * size)
        a = act(dot(k[:, cols], query[cols, :])).astype(BF)
        need("v")
        outs.append((dot(v[cols, :], a) * share).astype(BF))
    att = jnp.concatenate(outs, axis=0).astype(F32)
    need("wu")
    gate = project(wu, 1.0)
    mean = jnp.mean(att, axis=0, keepdims=True)
    cent = att - mean
    var = jnp.mean(cent * cent, axis=0, keepdims=True)
    gated = (cent * lax.rsqrt(var + 1e-06) * gate.astype(F32)).astype(BF)
    return jnp.sum(dot(vec[...], gated), axis=0, keepdims=True)


def rank_kernel(last, *refs):
    if last:
        length_ref, vec_ref, prev_ref, x_hbm, wq_hbm, wu_hbm, k_hbm, v_hbm, out_ref = refs[:9]
    else:
        length_ref, vec_ref, x_hbm, wq_hbm, wu_hbm, k_hbm, v_hbm, out_ref = refs[:8]
    x, wq, wu, k, v, sem = refs[-6:]
    cuts = [slice(i, i + TILE) for i in range(0, x.shape[0], TILE)]
    loads = [("x0", x_hbm.at[cuts[0], :], x.at[cuts[0], :]), ("wq", wq_hbm, wq)]
    loads += [("k", k_hbm, k), ("v", v_hbm, v), ("wu", wu_hbm, wu)]
    loads += [(f"x{i}", x_hbm.at[c, :], x.at[c, :]) for i, c in enumerate(cuts) if i > 0]
    left = {}
    for i, (name, a, b) in enumerate(loads):
        left[name] = pltpu.make_async_copy(a, b, sem.at[i])
        left[name].start()

    def need(name):
        if name in left:
            left.pop(name).wait()

    share = 1.0 / (length_ref[0] + NEW).astype(F32)
    for i, c in enumerate(cuts):
        need(f"x{i}")
        rows = x[c, :] if last else normalize(x[c, :].astype(F32)).astype(BF)
        line = rank_lines(share, rows, wq, wu, k, v, vec_ref, need)
        if not last:
            out_ref[:, c] = line
            continue
        odd = lax.rem(lax.broadcasted_iota(jnp.int32, (16, 128), 0), 2) == 1
        for j in range(TILE // 128):
            b = i * (TILE // 128) + j
            mine = line[:, j * 128 : (j + 1) * 128]
            early = prev_ref[:, b * 128 : (b + 1) * 128]
            out_ref[16 * b : 16 * (b + 1), :] = jnp.where(odd, mine, early)


def score_kernel(me_ref, place_ref, base_ref, ret_ref, out_ref):
    parties = ret_ref.shape[0] // 2
    rows = base_ref.shape[1]
    owner = place_ref[0:1, :]
    position = place_ref[1:2, :]
    half = position >= SLOTS
    at = 2 * owner + half.astype(jnp.int32)
    match = lax.broadcasted_iota(jnp.int32, (2 * parties, rows), 0) == at
    match = jnp.where(match, 1.0, 0.0).astype(BF)
    got = jnp.zeros((128, rows), F32)
    for part in split3(ret_ref[...]):
        got += dot(part, match, ((0,), (0,)))
    lane = position - jnp.where(half, SLOTS, 0) + lax.rem(me_ref[0], 128 // SLOTS) * SLOTS
    slot = lax.broadcasted_iota(jnp.int32, (128, rows), 0) == lane
    out_ref[...] = base_ref[...] + jnp.sum(jnp.where(slot, got, 0.0), axis=0, keepdims=True)


def whole(n):
    return [pl.BlockSpec(memory_space=pltpu.VMEM)] * n


def far(n):
    return [pl.BlockSpec(memory_space=pl.ANY)] * n


def small(n):
    return [pl.BlockSpec(memory_space=pltpu.SMEM)] * n


def params(limit=VMEM_LIMIT):
    return pltpu.CompilerParams(vmem_limit_bytes=limit)


def cost(macs, moved, transcendentals=0):
    return pl.CostEstimate(flops=2 * macs, bytes_accessed=moved, transcendentals=transcendentals)


def on_device(
    row_x, row_user, user_owner, hist_len, new_rows, cache_keys, cache_values, w_in, w_out, w_score
):
    n_own = lax.axis_size("own")
    rows, width = row_x.shape
    users = user_owner.shape[0]
    hist = cache_keys.shape[1]
    total = hist + NEW
    count = n_own * SLOTS
    score_row = w_score.reshape(1, width)
    sds = jax.ShapeDtypeStruct
    dma = pltpu.SemaphoreType.DMA

    def all_to_all(v):
        return lax.all_to_all(v, "own", split_axis=0, concat_axis=0, tiled=True)

    buf, place = pl.pallas_call(
        lambda *refs: route_kernel(SLOTS, *refs),
        out_shape=(sds((count, width), BF), sds((2, rows), jnp.int32)),
        in_specs=far(1) + whole(2),
        out_specs=(far(1)[0], whole(1)[0]),
        scratch_shapes=[
            pltpu.VMEM((rows, width), BF),
            pltpu.VMEM((count, width), BF),
            dma,
            dma((count // 256,)),
        ],
        compiler_params=params(),
        cost_estimate=cost(rows * width * count, 2 * 2 * rows * width),
        name="route",
    )(row_x, row_user.reshape(1, rows), user_owner.reshape(1, users))
    piece0 = all_to_all(buf.reshape(n_own, SLOTS, width)).reshape(count, width)

    keys, values, wq, wu, vec, new_out, buf, base = pl.pallas_call(
        lambda *refs: new_kernel(SLOTS, *refs),
        out_shape=(
            sds((total, width), BF),
            sds((width, total), BF),
            sds((width, width), BF),
            sds((width, width), BF),
            sds((8, width), BF),
            sds((NEW, width), BF),
            sds((count, width), BF),
            sds((1, rows), F32),
        ),
        in_specs=small(1) + whole(8),
        out_specs=tuple(whole(8)),
        scratch_shapes=[pltpu.VMEM((rows, width), BF)],
        compiler_params=params(),
        cost_estimate=cost(8 * NEW * width * width + rows * width * count, 24 * width * width),
        name="fresh",
    )(hist_len, new_rows[0], w_in, cache_keys[0], cache_values[0], w_out, score_row, row_x, place)
    piece1 = all_to_all(buf.reshape(n_own, SLOTS, width)).reshape(count, width)

    def rank(piece, prev):
        last = prev is not None
        return pl.pallas_call(
            lambda *refs: rank_kernel(last, *refs),
            out_shape=sds((2 * n_own, 128), F32) if last else sds((1, count), F32),
            in_specs=small(1) + whole(2 if last else 1) + far(5),
            out_specs=whole(1)[0],
            scratch_shapes=[
                pltpu.VMEM((count, width), BF),
                pltpu.VMEM((width, width), BF),
                pltpu.VMEM((width, width), BF),
                pltpu.VMEM((total, width), BF),
                pltpu.VMEM((width, total), BF),
                dma((4 + count // TILE,)),
            ],
            compiler_params=params(),
            cost_estimate=cost(
                count * width * (2 * width + 4 * total), 10 * width * width, count * HEADS * total
            ),
            name="rank",
        )(hist_len, vec, *([prev] if last else []), piece, wq, wu, keys, values)

    result = rank(piece1, rank(piece0, None))
    returned = all_to_all(result.reshape(n_own, 2, 128)).reshape(2 * n_own, 128)
    scores = pl.pallas_call(
        score_kernel,
        out_shape=sds((1, rows), F32),
        in_specs=small(1) + whole(3),
        out_specs=whole(1)[0],
        compiler_params=params(8 * 1024 * 1024),
        name="scores",
    )(lax.axis_index("own").reshape(1), place, base, returned)
    return (scores.reshape(rows), new_out[None])


def solution(mesh):
    placed = (
        P(("grp", "own"), None),
        P(("grp", "own"), None),
        P("grp"),
        P(("grp", "own")),
        P(("grp", "own"), None, None),
        P(("grp", "own"), None, None),
        P(("grp", "own"), None, None),
        P(),
        P(),
        P(),
    )
    return jax.shard_map(
        on_device,
        mesh=mesh,
        in_specs=placed,
        out_specs=(P(("grp", "own")), P(("grp", "own"), None, None)),
        check_vma=False,
    )
```

```python
import jax
import jax.numpy as jnp
from jax import lax
from jax.experimental import pallas as pl
from jax.experimental.pallas import tpu as pltpu
from jax.sharding import PartitionSpec as P

HEADS = 8
NEW = 64
BF = jnp.bfloat16
F32 = jnp.float32
VMEM_LIMIT = 56 * 1024 * 1024
SLOTS = 16
TILE = 512


def dot(a, b, dims=((1,), (0,))):
    return lax.dot_general(a, b, (dims, ((), ())), preferred_element_type=F32)


def normalize(v):
    mean = jnp.mean(v, axis=-1, keepdims=True)
    cent = v - mean
    var = jnp.mean(cent * cent, axis=-1, keepdims=True)
    return cent * lax.rsqrt(var + 1e-06)


def silu(v):
    half = 0.5 * v
    return half + half * jnp.tanh(half)


def split3(v):
    hi = v.astype(BF)
    rest = v - hi.astype(F32)
    mid = rest.astype(BF)
    low = (rest - mid.astype(F32)).astype(BF)
    return hi, mid, low


def split_rows(row):
    width = row.shape[1]
    hi, mid, low = split3(row)
    place = lax.broadcasted_iota(jnp.int32, (8, width), 0)
    parts = jnp.where(place == 0, hi.astype(F32), 0.0)
    parts = jnp.where(place == 1, mid.astype(F32), parts)
    return jnp.where(place == 2, low.astype(F32), parts).astype(BF)


def place_rows(user_ref, owner_ref, place_ref):
    rows = user_ref.shape[1]
    users = owner_ref.shape[1]
    step = 128
    along = lax.broadcasted_iota(jnp.int32, (users, users), 0)
    across = lax.broadcasted_iota(jnp.int32, (users, users), 1)
    owners = jnp.sum(
        jnp.where(along == across, owner_ref[...], 0).astype(F32), axis=1, keepdims=True
    )
    before = lax.broadcasted_iota(jnp.int32, (step, step), 0) < lax.broadcasted_iota(
        jnp.int32, (step, step), 1
    )
    before = jnp.where(before, 1.0, 0.0).astype(BF)
    seen = jnp.zeros((users, 1), F32)
    for b in range(rows // step):
        part = slice(b * step, (b + 1) * step)
        match = lax.broadcasted_iota(jnp.int32, (users, step), 0) == user_ref[:, part]
        match = jnp.where(match, 1.0, 0.0)
        earlier = dot(match.astype(BF), before) + seen
        seen = seen + jnp.sum(match, axis=1, keepdims=True)
        position = jnp.sum(earlier * match, axis=0, keepdims=True)
        owner = jnp.sum(owners * match, axis=0, keepdims=True)
        place_ref[0:1, part] = owner.astype(jnp.int32)
        place_ref[1:2, part] = position.astype(jnp.int32)


def fill(out_ref, slots, first, place_ref, normed_ref, done=None):
    rows = normed_ref.shape[0]
    owner = place_ref[0:1, :]
    position = place_ref[1:2, :]
    inside = jnp.logical_and(position >= first, position < first + slots)
    key = jnp.where(inside, owner * slots + position - first, -1)
    step = 256
    for b in range(out_ref.shape[0] // step):
        at = lax.broadcasted_iota(jnp.int32, (step, rows), 0) + b * step
        pick = jnp.where(at == key, 1.0, 0.0).astype(BF)
        out_ref[b * step : (b + 1) * step, :] = dot(pick, normed_ref[...]).astype(BF)
        if done is not None:
            done(b, slice(b * step, (b + 1) * step))


def route_kernel(slots, x_ref, user_ref, owner_ref, buf_ref, place_ref):
    place_rows(user_ref, owner_ref, place_ref)
    fill(buf_ref, slots, 0, place_ref, x_ref)


def fill_second(slots, first, x_ref, place_ref, score_ref, buf_ref, base_ref, normed_ref):
    rows = x_ref.shape[0]
    step = 128
    for b in range(rows // step):
        part = slice(b * step, (b + 1) * step)
        normed_ref[part, :] = normalize(x_ref[part, :].astype(F32)).astype(BF)
    base = dot(split_rows(score_ref[...]), x_ref[...], ((1,), (1,)))
    base_ref[...] = jnp.sum(base, axis=0, keepdims=True)
    fill(buf_ref, slots, first, place_ref, normed_ref)


def flip(v, scale=1.0):
    return jnp.transpose(v.astype(F32) * scale).astype(BF)


def new_kernel(
    slots, length_ref, new_ref, w_in_ref, keys_ref, values_ref, w_out_ref, score_ref, x_ref, place_ref,
    k_ref, v_ref, wq_ref, wu_ref, vec_ref, out_ref, buf_ref, base_ref, normed_ref,
):
    fill_second(slots, slots, x_ref, place_ref, score_ref, buf_ref, base_ref, normed_ref)
    length = length_ref[0]
    fresh, width = new_ref.shape
    hist = keys_ref.shape[0]
    size = width // HEADS
    step = 256
    rows = new_ref[...].astype(F32)
    normed = normalize(rows).astype(BF)
    cut = [
        silu(dot(normed, w_in_ref[:, i * width : (i + 1) * width])).astype(BF) for i in range(4)
    ]
    gate, value, query, key = cut
    k_ref[0:hist, :] = keys_ref[...]
    k_ref[hist : hist + fresh, :] = key
    for i in range(0, hist, step):
        kept = lax.broadcasted_iota(jnp.int32, (step, step), 0) + i < length
        for j in range(0, width, step):
            block = values_ref[i : i + step, j : j + step].astype(F32)
            v_ref[j : j + step, i : i + step] = flip(jnp.where(kept, block, 0.0))
    v_ref[:, hist : hist + fresh] = flip(value)
    for i in range(0, width, step):
        for j in range(0, width, step):
            wu_ref[j : j + step, i : i + step] = flip(w_in_ref[i : i + step, j : j + step], 0.5)
            wq_ref[j : j + step, i : i + step] = flip(
                w_in_ref[i : i + step, 2 * width + j : 2 * width + j + step], 0.5
            )
    vec = jnp.sum(dot(split_rows(score_ref[...]), w_out_ref[...], ((1,), (1,))), axis=0, keepdims=True)
    vec_ref[...] = split_rows(vec)
    total = hist + fresh
    at = lax.broadcasted_iota(jnp.int32, (fresh, total), 1)
    line = lax.broadcasted_iota(jnp.int32, (fresh, total), 0)
    keep = at <= line + hist
    outs = []
    for h in range(HEADS):
        cols = slice(h * size, (h + 1) * size)
        s = dot(query[:, cols], k_ref[:, cols], ((1,), (1,))) * (1.0 / size**0.5)
        a = jnp.where(keep, silu(s), 0.0).astype(BF)
        outs.append(dot(a, v_ref[cols, :], ((1,), (1,))))
    number = lax.broadcasted_iota(jnp.int32, (fresh, 1), 0) + (length + 1)
    att = (jnp.concatenate(outs, axis=1) / number.astype(F32)).astype(BF)
    gated = (normalize(att.astype(F32)) * gate.astype(F32)).astype(BF)
    out_ref[...] = (rows + dot(gated, w_out_ref[...])).astype(BF)


def rank_lines(share, x, wq, wu, k, v, vec, need):
    width = x.shape[1]
    size = width // HEADS
    step = 256

    def act(half):
        return half + half * jnp.tanh(half)

    def project(w, scale):
        parts = [dot(w[i : i + step, :], x, ((1,), (1,))) for i in range(0, width, step)]
        return jnp.concatenate([(act(p) * scale).astype(BF) for p in parts], axis=0)

    need("wq")
    query = project(wq, 0.5 / size**0.5)
    outs = []
    need("k")
    for h in range(HEADS):
        cols = slice(h * size, (h + 1) * size)
        a = act(dot(k[:, cols], query[cols, :])).astype(BF)
        need("v")
        outs.append((dot(v[cols, :], a) * share).astype(BF))
    att = jnp.concatenate(outs, axis=0).astype(F32)
    need("wu")
    gate = project(wu, 1.0)
    mean = jnp.mean(att, axis=0, keepdims=True)
    cent = att - mean
    var = jnp.mean(cent * cent, axis=0, keepdims=True)
    gated = (cent * lax.rsqrt(var + 1e-06) * gate.astype(F32)).astype(BF)
    return jnp.sum(dot(vec[...], gated), axis=0, keepdims=True)


def rank_kernel(last, *refs):
    if last:
        length_ref, vec_ref, prev_ref, x_hbm, wq_hbm, wu_hbm, k_hbm, v_hbm, out_ref = refs[:9]
    else:
        length_ref, vec_ref, x_hbm, wq_hbm, wu_hbm, k_hbm, v_hbm, out_ref = refs[:8]
    x, wq, wu, k, v, sem = refs[-6:]
    cuts = [slice(i, i + TILE) for i in range(0, x.shape[0], TILE)]
    loads = [("x0", x_hbm.at[cuts[0], :], x.at[cuts[0], :]), ("wq", wq_hbm, wq)]
    loads += [("k", k_hbm, k), ("v", v_hbm, v), ("wu", wu_hbm, wu)]
    loads += [(f"x{i}", x_hbm.at[c, :], x.at[c, :]) for i, c in enumerate(cuts) if i > 0]
    moves = {}
    for i, (name, a, b) in enumerate(loads):
        moves[name] = pltpu.make_async_copy(a, b, sem.at[i])
        moves[name].start()
    share = 1.0 / (length_ref[0] + NEW).astype(F32)
    line_ref = refs[-7]

    @pl.loop(0, len(cuts))
    def _(i):
        met = set()

        def need(name, at=0):
            if name not in met:
                met.add(name)
                pl.when(i == at)(moves[name].wait)

        for n in range(len(cuts)):
            need(f"x{n}", n)
        rows = x[pl.ds(pl.multiple_of(i * TILE, TILE), TILE), :]
        if not last:
            rows = normalize(rows.astype(F32)).astype(BF)
        line_ref[pl.ds(i, 1), :] = rank_lines(share, rows, wq, wu, k, v, vec_ref, need)

    odd = lax.rem(lax.broadcasted_iota(jnp.int32, (16, 128), 0), 2) == 1
    for i, c in enumerate(cuts):
        line = line_ref[i : i + 1, :]
        if not last:
            out_ref[:, c] = line
            continue
        for j in range(TILE // 128):
            b = i * (TILE // 128) + j
            mine = line[:, j * 128 : (j + 1) * 128]
            early = prev_ref[:, b * 128 : (b + 1) * 128]
            out_ref[16 * b : 16 * (b + 1), :] = jnp.where(odd, mine, early)


def score_kernel(me_ref, place_ref, base_ref, ret_ref, out_ref):
    parties = ret_ref.shape[0] // 2
    rows = base_ref.shape[1]
    owner = place_ref[0:1, :]
    position = place_ref[1:2, :]
    half = position >= SLOTS
    at = 2 * owner + half.astype(jnp.int32)
    match = lax.broadcasted_iota(jnp.int32, (2 * parties, rows), 0) == at
    match = jnp.where(match, 1.0, 0.0).astype(BF)
    got = jnp.zeros((128, rows), F32)
    for part in split3(ret_ref[...]):
        got += dot(part, match, ((0,), (0,)))
    lane = position - jnp.where(half, SLOTS, 0) + lax.rem(me_ref[0], 128 // SLOTS) * SLOTS
    slot = lax.broadcasted_iota(jnp.int32, (128, rows), 0) == lane
    out_ref[...] = base_ref[...] + jnp.sum(jnp.where(slot, got, 0.0), axis=0, keepdims=True)


def whole(n):
    return [pl.BlockSpec(memory_space=pltpu.VMEM)] * n


def far(n):
    return [pl.BlockSpec(memory_space=pl.ANY)] * n


def small(n):
    return [pl.BlockSpec(memory_space=pltpu.SMEM)] * n


def params(limit=VMEM_LIMIT):
    return pltpu.CompilerParams(vmem_limit_bytes=limit)


def cost(macs, moved, transcendentals=0):
    return pl.CostEstimate(flops=2 * macs, bytes_accessed=moved, transcendentals=transcendentals)


def on_device(
    row_x, row_user, user_owner, hist_len, new_rows, cache_keys, cache_values, w_in, w_out, w_score
):
    n_own = lax.axis_size("own")
    rows, width = row_x.shape
    users = user_owner.shape[0]
    hist = cache_keys.shape[1]
    total = hist + NEW
    count = n_own * SLOTS
    score_row = w_score.reshape(1, width)
    sds = jax.ShapeDtypeStruct
    dma = pltpu.SemaphoreType.DMA

    def all_to_all(v):
        return lax.all_to_all(v, "own", split_axis=0, concat_axis=0, tiled=True)

    buf, place = pl.pallas_call(
        lambda *refs: route_kernel(SLOTS, *refs),
        out_shape=(sds((count, width), BF), sds((2, rows), jnp.int32)),
        in_specs=whole(3),
        out_specs=tuple(whole(2)),
        compiler_params=params(),
        cost_estimate=cost(rows * width * count, 2 * 2 * rows * width),
        name="route",
    )(row_x, row_user.reshape(1, rows), user_owner.reshape(1, users))
    piece0 = all_to_all(buf.reshape(n_own, SLOTS, width)).reshape(count, width)

    keys, values, wq, wu, vec, new_out, buf, base = pl.pallas_call(
        lambda *refs: new_kernel(SLOTS, *refs),
        out_shape=(
            sds((total, width), BF),
            sds((width, total), BF),
            sds((width, width), BF),
            sds((width, width), BF),
            sds((8, width), BF),
            sds((NEW, width), BF),
            sds((count, width), BF),
            sds((1, rows), F32),
        ),
        in_specs=small(1) + whole(8),
        out_specs=tuple(whole(8)),
        scratch_shapes=[pltpu.VMEM((rows, width), BF)],
        compiler_params=params(),
        cost_estimate=cost(8 * NEW * width * width + rows * width * count, 24 * width * width),
        name="fresh",
    )(hist_len, new_rows[0], w_in, cache_keys[0], cache_values[0], w_out, score_row, row_x, place)
    piece1 = all_to_all(buf.reshape(n_own, SLOTS, width)).reshape(count, width)

    def rank(piece, prev):
        last = prev is not None
        return pl.pallas_call(
            lambda *refs: rank_kernel(last, *refs),
            out_shape=sds((2 * n_own, 128), F32) if last else sds((1, count), F32),
            in_specs=small(1) + whole(2 if last else 1) + far(5),
            out_specs=whole(1)[0],
            scratch_shapes=[
                pltpu.VMEM((count // TILE, TILE), F32),
                pltpu.VMEM((count, width), BF),
                pltpu.VMEM((width, width), BF),
                pltpu.VMEM((width, width), BF),
                pltpu.VMEM((total, width), BF),
                pltpu.VMEM((width, total), BF),
                dma((4 + count // TILE,)),
            ],
            compiler_params=params(),
            cost_estimate=cost(
                count * width * (2 * width + 4 * total), 10 * width * width, count * HEADS * total
            ),
            name="rank",
        )(hist_len, vec, *([prev] if last else []), piece, wq, wu, keys, values)

    result = rank(piece1, rank(piece0, None))
    returned = all_to_all(result.reshape(n_own, 2, 128)).reshape(2 * n_own, 128)
    scores = pl.pallas_call(
        score_kernel,
        out_shape=sds((1, rows), F32),
        in_specs=small(1) + whole(3),
        out_specs=whole(1)[0],
        compiler_params=params(8 * 1024 * 1024),
        name="scores",
    )(lax.axis_index("own").reshape(1), place, base, returned)
    return (scores.reshape(rows), new_out[None])


def solution(mesh):
    placed = (
        P(("grp", "own"), None),
        P(("grp", "own"), None),
        P("grp"),
        P(("grp", "own")),
        P(("grp", "own"), None, None),
        P(("grp", "own"), None, None),
        P(("grp", "own"), None, None),
        P(),
        P(),
        P(),
    )
    return jax.shard_map(
        on_device,
        mesh=mesh,
        in_specs=placed,
        out_specs=(P(("grp", "own")), P(("grp", "own"), None, None)),
        check_vma=False,
    )
```

```python
import jax
import jax.numpy as jnp
from jax import lax
from jax.experimental import pallas as pl
from jax.experimental.pallas import tpu as pltpu
from jax.sharding import PartitionSpec as P

HEADS = 8
NEW = 64
BF = jnp.bfloat16
F32 = jnp.float32
VMEM_LIMIT = 56 * 1024 * 1024
SLOTS = 16
TILE = 512


def dot(a, b, dims=((1,), (0,))):
    return lax.dot_general(a, b, (dims, ((), ())), preferred_element_type=F32)


def normalize(v):
    mean = jnp.mean(v, axis=-1, keepdims=True)
    cent = v - mean
    var = jnp.mean(cent * cent, axis=-1, keepdims=True)
    return cent * lax.rsqrt(var + 1e-06)


def silu(v):
    half = 0.5 * v
    return half + half * jnp.tanh(half)


def split3(v):
    hi = v.astype(BF)
    rest = v - hi.astype(F32)
    mid = rest.astype(BF)
    low = (rest - mid.astype(F32)).astype(BF)
    return hi, mid, low


def split_rows(row):
    width = row.shape[1]
    hi, mid, low = split3(row)
    place = lax.broadcasted_iota(jnp.int32, (8, width), 0)
    parts = jnp.where(place == 0, hi.astype(F32), 0.0)
    parts = jnp.where(place == 1, mid.astype(F32), parts)
    return jnp.where(place == 2, low.astype(F32), parts).astype(BF)


def place_rows(user_ref, owner_ref, place_ref):
    rows = user_ref.shape[1]
    users = owner_ref.shape[1]
    step = 128
    along = lax.broadcasted_iota(jnp.int32, (users, users), 0)
    across = lax.broadcasted_iota(jnp.int32, (users, users), 1)
    owners = jnp.sum(
        jnp.where(along == across, owner_ref[...], 0).astype(F32), axis=1, keepdims=True
    )
    before = lax.broadcasted_iota(jnp.int32, (step, step), 0) < lax.broadcasted_iota(
        jnp.int32, (step, step), 1
    )
    before = jnp.where(before, 1.0, 0.0).astype(BF)
    seen = jnp.zeros((users, 1), F32)
    for b in range(rows // step):
        part = slice(b * step, (b + 1) * step)
        match = lax.broadcasted_iota(jnp.int32, (users, step), 0) == user_ref[:, part]
        match = jnp.where(match, 1.0, 0.0)
        earlier = dot(match.astype(BF), before) + seen
        seen = seen + jnp.sum(match, axis=1, keepdims=True)
        position = jnp.sum(earlier * match, axis=0, keepdims=True)
        owner = jnp.sum(owners * match, axis=0, keepdims=True)
        place_ref[0:1, part] = owner.astype(jnp.int32)
        place_ref[1:2, part] = position.astype(jnp.int32)


def fill(out_ref, slots, first, place_ref, normed_ref, done=None):
    rows = normed_ref.shape[0]
    owner = place_ref[0:1, :]
    position = place_ref[1:2, :]
    inside = jnp.logical_and(position >= first, position < first + slots)
    key = jnp.where(inside, owner * slots + position - first, -1)
    step = 512
    at = lax.broadcasted_iota(jnp.int32, (step, rows), 0)
    for b in range(out_ref.shape[0] // step):
        pick = jnp.where(at == key - b * step, 1.0, 0.0).astype(BF)
        out_ref[b * step : (b + 1) * step, :] = dot(pick, normed_ref[...]).astype(BF)
        if done is not None:
            done(b, slice(b * step, (b + 1) * step))


def route_kernel(slots, x_ref, user_ref, owner_ref, buf_ref, place_ref):
    place_rows(user_ref, owner_ref, place_ref)
    fill(buf_ref, slots, 0, place_ref, x_ref)


def fill_second(slots, first, x_ref, place_ref, score_ref, buf_ref, base_ref, normed_ref):
    rows = x_ref.shape[0]
    step = 128
    for b in range(rows // step):
        part = slice(b * step, (b + 1) * step)
        normed_ref[part, :] = normalize(x_ref[part, :].astype(F32)).astype(BF)
    base = dot(split_rows(score_ref[...]), x_ref[...], ((1,), (1,)))
    base_ref[...] = jnp.sum(base, axis=0, keepdims=True)
    fill(buf_ref, slots, first, place_ref, normed_ref)


def flip(v, scale=1.0):
    return jnp.transpose(v.astype(F32) * scale).astype(BF)


def new_kernel(
    slots, length_ref, new_ref, w_in_ref, keys_ref, values_ref, w_out_ref, score_ref, x_ref, place_ref,
    k_ref, v_ref, wq_ref, wu_ref, vec_ref, out_ref, buf_ref, base_ref, normed_ref,
):
    fill_second(slots, slots, x_ref, place_ref, score_ref, buf_ref, base_ref, normed_ref)
    length = length_ref[0]
    fresh, width = new_ref.shape
    hist = keys_ref.shape[0]
    size = width // HEADS
    step = 256
    rows = new_ref[...].astype(F32)
    normed = normalize(rows).astype(BF)
    cut = [
        silu(dot(normed, w_in_ref[:, i * width : (i + 1) * width])).astype(BF) for i in range(4)
    ]
    gate, value, query, key = cut
    k_ref[0:hist, :] = keys_ref[...]
    k_ref[hist : hist + fresh, :] = key
    for i in range(0, hist, step):
        kept = lax.broadcasted_iota(jnp.int32, (step, step), 0) + i < length
        for j in range(0, width, step):
            block = values_ref[i : i + step, j : j + step].astype(F32)
            v_ref[j : j + step, i : i + step] = flip(jnp.where(kept, block, 0.0))
    v_ref[:, hist : hist + fresh] = flip(value)
    for i in range(0, width, step):
        for j in range(0, width, step):
            wu_ref[j : j + step, i : i + step] = flip(w_in_ref[i : i + step, j : j + step], 0.5)
            wq_ref[j : j + step, i : i + step] = flip(
                w_in_ref[i : i + step, 2 * width + j : 2 * width + j + step], 0.5
            )
    vec = jnp.sum(dot(split_rows(score_ref[...]), w_out_ref[...], ((1,), (1,))), axis=0, keepdims=True)
    vec_ref[...] = split_rows(vec)
    total = hist + fresh
    at = lax.broadcasted_iota(jnp.int32, (fresh, total), 1)
    line = lax.broadcasted_iota(jnp.int32, (fresh, total), 0)
    keep = at <= line + hist
    outs = []
    for h in range(HEADS):
        cols = slice(h * size, (h + 1) * size)
        s = dot(query[:, cols], k_ref[:, cols], ((1,), (1,))) * (1.0 / size**0.5)
        a = jnp.where(keep, silu(s), 0.0).astype(BF)
        outs.append(dot(a, v_ref[cols, :], ((1,), (1,))))
    number = lax.broadcasted_iota(jnp.int32, (fresh, 1), 0) + (length + 1)
    att = (jnp.concatenate(outs, axis=1) / number.astype(F32)).astype(BF)
    gated = (normalize(att.astype(F32)) * gate.astype(F32)).astype(BF)
    out_ref[...] = (rows + dot(gated, w_out_ref[...])).astype(BF)


def rank_lines(share, x, wq, wu, k, v, vec, need):
    width = x.shape[1]
    size = width // HEADS
    step = 256

    def act(half):
        return half + half * jnp.tanh(half)

    def project(w, scale):
        parts = [dot(w[i : i + step, :], x, ((1,), (1,))) for i in range(0, width, step)]
        return jnp.concatenate([(act(p) * scale).astype(BF) for p in parts], axis=0)

    need("wq")
    query = project(wq, 0.5 / size**0.5)
    outs = []
    need("k")
    for h in range(HEADS):
        cols = slice(h * size, (h + 1) * size)
        a = act(dot(k[:, cols], query[cols, :])).astype(BF)
        need("v")
        outs.append((dot(v[cols, :], a) * share).astype(BF))
    att = jnp.concatenate(outs, axis=0).astype(F32)
    need("wu")
    gate = project(wu, 1.0)
    mean = jnp.mean(att, axis=0, keepdims=True)
    cent = att - mean
    var = jnp.mean(cent * cent, axis=0, keepdims=True)
    gated = (cent * lax.rsqrt(var + 1e-06) * gate.astype(F32)).astype(BF)
    return jnp.sum(dot(vec[...], gated), axis=0, keepdims=True)


def rank_kernel(last, *refs):
    if last:
        length_ref, vec_ref, prev_ref, x_hbm, wq_hbm, wu_hbm, k_hbm, v_hbm, out_ref = refs[:9]
    else:
        length_ref, vec_ref, x_hbm, wq_hbm, wu_hbm, k_hbm, v_hbm, out_ref = refs[:8]
    x, wq, wu, k, v, sem = refs[-6:]
    cuts = [slice(i, i + TILE) for i in range(0, x.shape[0], TILE)]
    loads = [("x0", x_hbm.at[cuts[0], :], x.at[cuts[0], :]), ("wq", wq_hbm, wq)]
    loads += [("k", k_hbm, k), ("v", v_hbm, v), ("wu", wu_hbm, wu)]
    loads += [(f"x{i}", x_hbm.at[c, :], x.at[c, :]) for i, c in enumerate(cuts) if i > 0]
    moves = {}
    for i, (name, a, b) in enumerate(loads):
        moves[name] = pltpu.make_async_copy(a, b, sem.at[i])
        moves[name].start()
    share = 1.0 / (length_ref[0] + NEW).astype(F32)
    line_ref = refs[-7]

    @pl.loop(0, len(cuts))
    def _(i):
        met = set()

        def need(name, at=0):
            if name not in met:
                met.add(name)
                pl.when(i == at)(moves[name].wait)

        for n in range(len(cuts)):
            need(f"x{n}", n)
        rows = x[pl.ds(pl.multiple_of(i * TILE, TILE), TILE), :]
        if not last:
            rows = normalize(rows.astype(F32)).astype(BF)
        line_ref[pl.ds(i, 1), :] = rank_lines(share, rows, wq, wu, k, v, vec_ref, need)

    odd = lax.rem(lax.broadcasted_iota(jnp.int32, (16, 128), 0), 2) == 1
    for i, c in enumerate(cuts):
        line = line_ref[i : i + 1, :]
        if not last:
            out_ref[:, c] = line
            continue
        for j in range(TILE // 128):
            b = i * (TILE // 128) + j
            mine = line[:, j * 128 : (j + 1) * 128]
            early = prev_ref[:, b * 128 : (b + 1) * 128]
            out_ref[16 * b : 16 * (b + 1), :] = jnp.where(odd, mine, early)


def score_kernel(me_ref, place_ref, base_ref, ret_ref, out_ref):
    parties = ret_ref.shape[0] // 2
    rows = base_ref.shape[1]
    owner = place_ref[0:1, :]
    position = place_ref[1:2, :]
    half = position >= SLOTS
    at = 2 * owner + half.astype(jnp.int32)
    match = lax.broadcasted_iota(jnp.int32, (2 * parties, rows), 0) == at
    match = jnp.where(match, 1.0, 0.0).astype(BF)
    got = jnp.zeros((128, rows), F32)
    for part in split3(ret_ref[...]):
        got += dot(part, match, ((0,), (0,)))
    lane = position - jnp.where(half, SLOTS, 0) + lax.rem(me_ref[0], 128 // SLOTS) * SLOTS
    slot = lax.broadcasted_iota(jnp.int32, (128, rows), 0) == lane
    out_ref[...] = base_ref[...] + jnp.sum(jnp.where(slot, got, 0.0), axis=0, keepdims=True)


def whole(n):
    return [pl.BlockSpec(memory_space=pltpu.VMEM)] * n


def far(n):
    return [pl.BlockSpec(memory_space=pl.ANY)] * n


def small(n):
    return [pl.BlockSpec(memory_space=pltpu.SMEM)] * n


def params(limit=VMEM_LIMIT):
    return pltpu.CompilerParams(vmem_limit_bytes=limit)


def cost(macs, moved, transcendentals=0):
    return pl.CostEstimate(flops=2 * macs, bytes_accessed=moved, transcendentals=transcendentals)


def on_device(
    row_x, row_user, user_owner, hist_len, new_rows, cache_keys, cache_values, w_in, w_out, w_score
):
    n_own = lax.axis_size("own")
    rows, width = row_x.shape
    users = user_owner.shape[0]
    hist = cache_keys.shape[1]
    total = hist + NEW
    count = n_own * SLOTS
    score_row = w_score.reshape(1, width)
    sds = jax.ShapeDtypeStruct
    dma = pltpu.SemaphoreType.DMA

    def all_to_all(v):
        return lax.all_to_all(v, "own", split_axis=0, concat_axis=0, tiled=True)

    buf, place = pl.pallas_call(
        lambda *refs: route_kernel(SLOTS, *refs),
        out_shape=(sds((count, width), BF), sds((2, rows), jnp.int32)),
        in_specs=whole(3),
        out_specs=tuple(whole(2)),
        compiler_params=params(),
        cost_estimate=cost(rows * width * count, 2 * 2 * rows * width),
        name="route",
    )(row_x, row_user.reshape(1, rows), user_owner.reshape(1, users))
    piece0 = all_to_all(buf.reshape(n_own, SLOTS, width)).reshape(count, width)

    keys, values, wq, wu, vec, new_out, buf, base = pl.pallas_call(
        lambda *refs: new_kernel(SLOTS, *refs),
        out_shape=(
            sds((total, width), BF),
            sds((width, total), BF),
            sds((width, width), BF),
            sds((width, width), BF),
            sds((8, width), BF),
            sds((NEW, width), BF),
            sds((count, width), BF),
            sds((1, rows), F32),
        ),
        in_specs=small(1) + whole(8),
        out_specs=tuple(whole(8)),
        scratch_shapes=[pltpu.VMEM((rows, width), BF)],
        compiler_params=params(),
        cost_estimate=cost(8 * NEW * width * width + rows * width * count, 24 * width * width),
        name="fresh",
    )(hist_len, new_rows[0], w_in, cache_keys[0], cache_values[0], w_out, score_row, row_x, place)
    piece1 = all_to_all(buf.reshape(n_own, SLOTS, width)).reshape(count, width)

    def rank(piece, prev):
        last = prev is not None
        return pl.pallas_call(
            lambda *refs: rank_kernel(last, *refs),
            out_shape=sds((2 * n_own, 128), F32) if last else sds((1, count), F32),
            in_specs=small(1) + whole(2 if last else 1) + far(5),
            out_specs=whole(1)[0],
            scratch_shapes=[
                pltpu.VMEM((count // TILE, TILE), F32),
                pltpu.VMEM((count, width), BF),
                pltpu.VMEM((width, width), BF),
                pltpu.VMEM((width, width), BF),
                pltpu.VMEM((total, width), BF),
                pltpu.VMEM((width, total), BF),
                dma((4 + count // TILE,)),
            ],
            compiler_params=params(),
            cost_estimate=cost(
                count * width * (2 * width + 4 * total), 10 * width * width, count * HEADS * total
            ),
            name="rank",
        )(hist_len, vec, *([prev] if last else []), piece, wq, wu, keys, values)

    result = rank(piece1, rank(piece0, None))
    returned = all_to_all(result.reshape(n_own, 2, 128)).reshape(2 * n_own, 128)
    scores = pl.pallas_call(
        score_kernel,
        out_shape=sds((1, rows), F32),
        in_specs=small(1) + whole(3),
        out_specs=whole(1)[0],
        compiler_params=params(8 * 1024 * 1024),
        name="scores",
    )(lax.axis_index("own").reshape(1), place, base, returned)
    return (scores.reshape(rows), new_out[None])


def solution(mesh):
    placed = (
        P(("grp", "own"), None),
        P(("grp", "own"), None),
        P("grp"),
        P(("grp", "own")),
        P(("grp", "own"), None, None),
        P(("grp", "own"), None, None),
        P(("grp", "own"), None, None),
        P(),
        P(),
        P(),
    )
    return jax.shard_map(
        on_device,
        mesh=mesh,
        in_specs=placed,
        out_specs=(P(("grp", "own")), P(("grp", "own"), None, None)),
        check_vma=False,
    )
```
